256 devices in a mesh: replica: 8 (over y, core), tensor: 32 (over x, z).
Axes of the slice: x: 4, y: 4, z: 8, core: 2. Of those that a mesh axis runs over, the one named last changes fastest.
Arguments:
- tokens: bfloat16 [1024, 2560], P('replica', 'tensor'), may hold values from -6 to 6
- next_tokens: bfloat16 [512, 2560], P('replica', 'tensor'), may hold values from -6 to 6
- cotangent: bfloat16 [1024, 2560], P('replica', 'tensor'), may hold values from -0.5 to 0.5
- gate_weight: bfloat16 [2560, 14336], P(None, 'tensor'), may hold values from -0.125 to 0.125
- up_weight: bfloat16 [2560, 14336], P(None, 'tensor'), may hold values from -0.125 to 0.125
- down_weight: bfloat16 [14336, 2560], P('tensor'), may hold values from -0.046875 to 0.046875
- momentum: bfloat16 [8, 14336, 2560], P('replica', 'tensor'), may hold values from -6 to 6
- indices: int32 [8, 224, 40, 32], P(None, 'tensor'), may hold values from 0 to 4095, as said below
Outputs:
- output: bfloat16 [512, 2560], P(('replica', 'tensor'))
- new_momentum: bfloat16 [8, 14336, 2560], P('replica', 'tensor')
The draws below stay inside these ranges and needn't reach their ends.
Inputs may be any that keep to these rules, and one draw needn't show every extreme that they name: Within one replica and tile the 32 indices are distinct; the n-th lies in the range from n * 64 * 2 to (n + 1) * 64 * 2 - 1.
All inputs are finite; a program needn't handle non-finite values.
Results may differ from the reference program's by a relative error of at most 0.017.
Values may be sent and summed in bfloat16 or wider, within the bound.
No kernel may reach another device: no remote copies, remote signals or barrier semaphores. Data moves between devices by JAX's collectives and lax.ppermute only.
A program may use at most 128 MiB of HBM per device.

```python
import jax
import jax.numpy as jnp
from jax import lax

D = 2560
FF = 14336
TILE = 64
KEEP = 32
TOK = 128
REPLICAS = 8
TOKENS = 1024
NEXTS = 512


def draw_indices(key, part):
    stride = TILE * TILE // KEEP
    shape = (REPLICAS, FF // TILE, D // TILE, KEEP)
    offsets = jax.random.randint(key, shape, 0, stride, dtype=jnp.int32)
    base = jnp.arange(KEEP, dtype=jnp.int32) * stride
    return (offsets + base).astype(jnp.int32)


def levels(rng, extent, split, smallest, largest):
    def one(position, blocks):
        steps = jax.random.uniform(jax.random.fold_in(jax.random.fold_in(rng, 6), position), (blocks,), jnp.float32, smallest / len(split), largest / len(split))
        return jnp.repeat(jnp.exp(steps), extent[position] // blocks).reshape((-1,) + (1,) * (len(extent) - position - 1))

    factor_of = one(*split[0])
    for cut in split[1:]:
        factor_of = factor_of * one(*cut)
    return factor_of


def scatter_about(rng, shape, width, bound, cuts=(), kind=jnp.bfloat16):
    entries = width * jax.random.normal(rng, shape, jnp.float32)
    if cuts:
        entries = entries * levels(rng, shape, cuts, -0.22, 0.18)
    return jnp.clip(entries, -bound, bound).astype(kind)


def setup_inputs(seed: int = 0) -> dict:
    key_list = jax.random.split(jax.random.key(seed), 9)
    return {
        "tokens": scatter_about(key_list[0], (TOKENS, D), 1.0, 6.0, ((0, 8), (1, 32))),
        "next_tokens": scatter_about(key_list[1], (NEXTS, D), 1.0, 6.0, ((0, 8), (1, 32))),
        "cotangent": scatter_about(key_list[2], (TOKENS, D), 0.07, 0.5, ((0, 8), (1, 32))),
        "gate_weight": scatter_about(key_list[3], (D, FF), D ** -0.5, 0.125, ((1, 32),)),
        "up_weight": scatter_about(key_list[4], (D, FF), D ** -0.5, 0.125, ((1, 32),)),
        "down_weight": scatter_about(key_list[5], (FF, D), FF ** -0.5, 0.046875, ((0, 32),)),
        "momentum": scatter_about(key_list[6], (REPLICAS, FF, D), 1.0, 6.0, ((0, 8), (1, 32))),
        "indices": draw_indices(jax.random.fold_in(key_list[8], 71), 0),
    }


BETA_DECAY = 0.9
STEP_RATE = 0.1

def cosine_table():
    freq = jnp.arange(TILE, dtype=jnp.float32)[:, None]
    place = jnp.arange(TILE, dtype=jnp.float32)[None, :]
    table = jnp.cos(jnp.pi * (2.0 * place + 1.0) * freq / (2.0 * TILE))
    factor = jnp.where(freq == 0.0, jnp.sqrt(1.0 / TILE), jnp.sqrt(2.0 / TILE))
    return (table * factor).astype(jnp.float32)

def forward_tiles(field, table):
    height, breadth = field.shape
    blocks = field.reshape(height // TILE, TILE, breadth // TILE, TILE)
    spectrum = jnp.einsum('ak,xkyl,bl->xyab', table, blocks, table, precision=lax.Precision.HIGHEST)
    return spectrum.reshape(height // TILE, breadth // TILE, TILE * TILE)

def inverse_tiles(spectrum, table):
    tile_rows, tile_cols, _ = spectrum.shape
    blocks = spectrum.reshape(tile_rows, tile_cols, TILE, TILE)
    field = jnp.einsum('ak,xyab,bl->xkyl', table, blocks, table, precision=lax.Precision.HIGHEST)
    return field.reshape(tile_rows * TILE, tile_cols * TILE)

def place_values(values, where):
    tile_rows, tile_cols, _ = where.shape
    dense = jnp.zeros((tile_rows, tile_cols, TILE * TILE), jnp.float32)
    row_ids = jnp.arange(tile_rows, dtype=jnp.int32)[:, None, None]
    col_ids = jnp.arange(tile_cols, dtype=jnp.int32)[None, :, None]
    return dense.at[row_ids, col_ids, where].add(values)

def swiglu(inputs, gate_weight, up_weight):
    gate = jnp.dot(inputs, gate_weight, preferred_element_type=jnp.float32)
    upper = jnp.dot(inputs, up_weight, preferred_element_type=jnp.float32)
    return (jax.nn.silu(gate) * upper).astype(jnp.bfloat16)

def reference(tokens, next_tokens, cotangent, gate_weight, up_weight, down_weight, momentum, indices):
    table = cosine_table()

    def one_replica(replica):
        start = replica * TOK
        inputs = lax.dynamic_slice_in_dim(tokens, start, TOK, 0)
        grads_out = lax.dynamic_slice_in_dim(cotangent, start, TOK, 0)
        hidden = swiglu(inputs, gate_weight, up_weight)
        grad = jnp.dot(hidden.T, grads_out, preferred_element_type=jnp.float32)
        moment = BETA_DECAY * momentum[replica].astype(jnp.float32) + grad
        spectrum = forward_tiles(moment, table)
        where = indices[replica]
        sent = jnp.take_along_axis(spectrum, where, axis=2).astype(jnp.bfloat16)
        own = place_values(sent.astype(jnp.float32), where)
        kept = (moment - inverse_tiles(own, table)).astype(jnp.bfloat16)
        return (sent, kept)
    sent_all, new_momentum = lax.map(one_replica, jnp.arange(REPLICAS, dtype=jnp.int32))
    where_all = jnp.moveaxis(indices, 0, 2).reshape(FF // TILE, D // TILE, REPLICAS * KEEP)
    values_all = jnp.moveaxis(sent_all.astype(jnp.float32), 0, 2).reshape(FF // TILE, D // TILE, REPLICAS * KEEP)
    total = place_values(values_all, where_all)
    update = inverse_tiles(total, table) / REPLICAS
    new_down = (down_weight.astype(jnp.float32) - STEP_RATE * update).astype(jnp.bfloat16)
    next_hidden = swiglu(next_tokens, gate_weight, up_weight)
    output = jnp.dot(next_hidden, new_down, preferred_element_type=jnp.float32).astype(jnp.bfloat16)
    return (output, new_momentum)
```

```python
import functools

import jax
import jax.numpy as jnp
import ml_dtypes
import numpy as np
from jax import lax
from jax.experimental import pallas as pl
from jax.experimental.pallas import tpu as pltpu
from jax.sharding import PartitionSpec as P

TILE = 64
BETA_DECAY = 0.9
STEP_RATE = 0.1
BAND = 256
HALF = 256
VMEM = pl.BlockSpec(memory_space=pltpu.VMEM)
F32 = jnp.float32
BF16 = jnp.bfloat16


def cosine_table():
    freq = np.arange(TILE, dtype=np.float64)[:, None]
    place = np.arange(TILE, dtype=np.float64)[None, :]
    table = np.cos(np.pi * (2.0 * place + 1.0) * freq / (2.0 * TILE))
    return table * np.where(freq == 0.0, np.sqrt(1.0 / TILE), np.sqrt(2.0 / TILE))


def parts(table):
    high = table.astype(np.float32).astype(ml_dtypes.bfloat16)
    low = (table - high.astype(np.float64)).astype(np.float32).astype(ml_dtypes.bfloat16)
    return high, low


def row_table(rows):
    cosine = cosine_table()
    table = np.zeros((rows, 2 * HALF))
    for i in range(rows // TILE):
        for p in range(2):
            lanes = slice(p * HALF + i * (TILE // 2), p * HALF + (i + 1) * (TILE // 2))
            table[i * TILE : (i + 1) * TILE, lanes] = cosine[p::2].T
    return table


def band_table():
    return np.kron(np.eye(BAND // TILE), cosine_table())


def split(value):
    high = value.astype(BF16)
    return high, (value - high.astype(F32)).astype(BF16)


def dot(a, b):
    return jnp.dot(a, b, preferred_element_type=F32)


def dot3(a, b):
    return dot(a[0], b[0]) + (dot(a[1], b[0]) + dot(a[0], b[1]))


def momentum_spectrum_kernel(momentum, rows_high, rows_low, band_high, band_low, out):
    turned = momentum[0].T
    along = split(dot(turned, rows_high[...]) + dot(turned, rows_low[...]))
    out[...] = dot3((band_high[...], band_low[...]), along)


def spread(offsets, values, tile):
    column = lax.broadcasted_iota(jnp.int32, (TILE, HALF), 0)
    even = jnp.where(offsets == column, values, 0.0)
    odd = jnp.where(offsets == column + TILE, values, 0.0)
    return even, odd


def pick_kernel(cotangent, hidden_high, hidden_low, band_high, band_low, spectrum, offsets, out):
    turned = cotangent[...]
    grads = split(dot(band_high[...], turned) + dot(band_low[...], turned))
    whole = spectrum[...] + dot3(grads, (hidden_high[...], hidden_low[...]))
    column = lax.broadcasted_iota(jnp.int32, (TILE, HALF), 0)
    step = pl.program_id(0)
    tiles = BAND // TILE
    for k in range(tiles):
        spots = offsets[pl.ds(step * tiles + k, 1), :]
        even = whole[k * TILE : (k + 1) * TILE, :HALF]
        odd = whole[k * TILE : (k + 1) * TILE, HALF:]
        hit = jnp.where(spots == column, even, jnp.where(spots == column + TILE, odd, 0.0))
        out[pl.ds(step * tiles + k, 1), :] = jnp.sum(hit, axis=0, keepdims=True)


def output_kernel(values, offsets, next_rows, base, back_high, back_low, out, dense, listed):
    step = pl.program_id(0)
    tiles = BAND // TILE
    replicas = values.shape[0]

    @pl.when(step == 0)
    def _():
        listed[...] = values[...].astype(F32)

    column = lax.broadcasted_iota(jnp.int32, (TILE, HALF), 0)
    for k in range(tiles):
        even = jnp.zeros((TILE, HALF), F32)
        odd = jnp.zeros((TILE, HALF), F32)
        for r in range(replicas):
            spots = offsets[r, pl.ds(step * tiles + k, 1), :]
            value = listed[r, pl.ds(step * tiles + k, 1), :]
            even += jnp.where(spots == column, value, 0.0)
            odd += jnp.where(spots == column + TILE, value, 0.0)
        dense[k * TILE : (k + 1) * TILE, :HALF] = even.astype(BF16)
        dense[k * TILE : (k + 1) * TILE, HALF:] = odd.astype(BF16)
    both = dot(dense[...], next_rows[...])
    tokens = both.shape[1] // 2
    folded = both[:, :tokens] + both[:, tokens:]
    change = dot3((back_high[...], back_low[...]), split(folded))
    out[...] = (base[...] - (STEP_RATE / replicas) * change.T).astype(BF16)


def kept_kernel(sent, offsets, cotangent, hidden, momentum, back_high, back_low, rows_high, rows_low, out, dense):
    step = pl.program_id(0)
    tiles = BAND // TILE
    column = lax.broadcasted_iota(jnp.int32, (TILE, HALF), 0)
    for k in range(tiles):
        spots = offsets[pl.ds(step * tiles + k, 1), :]
        value = sent[pl.ds(step * tiles + k, 1), :]
        dense[k * TILE : (k + 1) * TILE, :HALF] = jnp.where(spots == column, value, 0.0).astype(BF16)
        dense[k * TILE : (k + 1) * TILE, HALF:] = jnp.where(spots == column + TILE, value, 0.0).astype(BF16)
    own = dense[...]
    along = split(dot(back_high[...], own) + dot(back_low[...], own))
    change = dot(cotangent[...], hidden[...]) - dot3(along, (rows_high[...], rows_low[...]))
    out[0] = (BETA_DECAY * momentum[0].astype(F32) + change.T).astype(BF16)


def whole_block(shape):
    return pl.BlockSpec(shape, lambda step: (0,) * len(shape))


def params():
    return pltpu.CompilerParams(dimension_semantics=("arbitrary",), vmem_limit_bytes=32 * 1024 * 1024)


def gather_rows(block, count):
    blocks = jnp.broadcast_to(block[None], (count,) + block.shape)
    return lax.all_to_all(blocks, "tensor", 0, 0, tiled=True).reshape(-1, block.shape[1])


def project(turned, weight):
    return lax.dot_general(turned, weight, (((0,), (0,)), ((), ())), preferred_element_type=F32)


def swiglu(turned, gate_weight, up_weight):
    return (jax.nn.silu(project(turned, gate_weight)) * project(turned, up_weight)).astype(BF16)


def on_device(tokens, next_tokens, cotangent, gate_weight, up_weight, down_weight, momentum, indices):
    shards = lax.axis_size("tensor")
    replicas = lax.axis_size("replica")
    replica = lax.axis_index("replica")
    rows, width = down_weight.shape
    bands = width // BAND
    tile_rows, tile_cols, keep = indices.shape[1:]
    stride = TILE * TILE // keep

    table = row_table(rows)
    rows_high, rows_low = parts(table)
    decayed_high, decayed_low = parts(BETA_DECAY * table)
    rows_back_high, rows_back_low = parts(table.T)
    band_high, band_low = parts(band_table())
    back_high, back_low = parts(band_table().T)

    offsets = indices - jnp.arange(keep, dtype=jnp.int32) * stride
    offsets = offsets.transpose(0, 2, 1, 3).reshape(replicas, tile_cols, tile_rows * keep)
    offsets = jnp.pad(offsets, ((0, 0), (0, 0), (0, HALF - tile_rows * keep)), constant_values=-1)
    own_offsets = lax.dynamic_index_in_dim(offsets, replica, 0, keepdims=False)

    count = tokens.shape[0]
    momentum_spectrum = pl.pallas_call(
        momentum_spectrum_kernel,
        grid=(bands,),
        in_specs=[pl.BlockSpec((1, rows, BAND), lambda step: (0, 0, step))]
        + [whole_block((rows, 2 * HALF))] * 2
        + [whole_block((BAND, BAND))] * 2,
        out_specs=pl.BlockSpec((BAND, 2 * HALF), lambda step: (step, 0)),
        out_shape=jax.ShapeDtypeStruct((width, 2 * HALF), F32),
        compiler_params=params(),
        cost_estimate=pl.CostEstimate(flops=9_000_000_000, bytes_accessed=8_000_000, transcendentals=0),
        name="momentum_spectrum",
    )(momentum, decayed_high, decayed_low, band_high, band_low)

    whole = gather_rows(tokens.T, shards)
    whole_grads = gather_rows(cotangent.T, shards)
    whole_next = gather_rows(next_tokens.T, shards)

    hidden = swiglu(whole, gate_weight, up_weight)
    hidden_high, hidden_low = split(dot(hidden, rows_high) + dot(hidden, rows_low))

    sent = pl.pallas_call(
        pick_kernel,
        grid=(bands,),
        in_specs=[pl.BlockSpec((BAND, count), lambda step: (step, 0))]
        + [whole_block((count, 2 * HALF))] * 2
        + [whole_block((BAND, BAND))] * 2
        + [pl.BlockSpec((BAND, 2 * HALF), lambda step: (step, 0)), whole_block((tile_cols, HALF))],
        out_specs=whole_block((tile_cols, HALF)),
        out_shape=jax.ShapeDtypeStruct((tile_cols, HALF), F32),
        compiler_params=params(),
        cost_estimate=pl.CostEstimate(flops=2_000_000_000, bytes_accessed=6_000_000, transcendentals=0),
        name="pick",
    )(whole_grads, hidden_high, hidden_low, band_high, band_low, momentum_spectrum, own_offsets)
    sent = sent.astype(BF16)

    listed = lax.all_to_all(
        jnp.broadcast_to(sent.reshape(-1, 128)[None], (replicas, sent.size // 128, 128)), "replica", 0, 0, tiled=True
    ).reshape(replicas, tile_cols, HALF)

    next_hidden = swiglu(whole_next, gate_weight, up_weight)
    base = dot(next_hidden, down_weight)
    next_rows = jnp.concatenate(split((dot(next_hidden, rows_high) + dot(next_hidden, rows_low)).T), axis=1)
    next_count = next_tokens.shape[0]

    partial = pl.pallas_call(
        output_kernel,
        grid=(bands,),
        in_specs=[
            whole_block((replicas, tile_cols, HALF)),
            whole_block((replicas, tile_cols, HALF)),
            whole_block((2 * HALF, 2 * next_count)),
            pl.BlockSpec((next_count, BAND), lambda step: (0, step)),
            whole_block((BAND, BAND)),
            whole_block((BAND, BAND)),
        ],
        out_specs=pl.BlockSpec((next_count, BAND), lambda step: (0, step)),
        out_shape=jax.ShapeDtypeStruct((next_count, width), BF16),
        scratch_shapes=[pltpu.VMEM((BAND, 2 * HALF), BF16), pltpu.VMEM((replicas, tile_cols, HALF), F32)],
        compiler_params=params(),
        cost_estimate=pl.CostEstimate(flops=3_000_000_000, bytes_accessed=2_000_000, transcendentals=0),
        name="output_part",
    )(listed, offsets, next_rows, base, back_high, back_low)

    pieces = lax.all_to_all(partial.reshape(shards, -1, 128), "tensor", 0, 0, tiled=True)
    output = jnp.sum(pieces.astype(F32), axis=0).astype(BF16).reshape(next_count // shards, width)

    kept = pl.pallas_call(
        kept_kernel,
        grid=(bands,),
        in_specs=[
            whole_block((tile_cols, HALF)),
            whole_block((tile_cols, HALF)),
            pl.BlockSpec((BAND, count), lambda step: (step, 0)),
            whole_block((count, rows)),
            pl.BlockSpec((1, rows, BAND), lambda step: (0, 0, step)),
            whole_block((BAND, BAND)),
            whole_block((BAND, BAND)),
            whole_block((2 * HALF, rows)),
            whole_block((2 * HALF, rows)),
        ],
        out_specs=pl.BlockSpec((1, rows, BAND), lambda step: (0, 0, step)),
        out_shape=jax.ShapeDtypeStruct((1, rows, width), BF16),
        scratch_shapes=[pltpu.VMEM((BAND, 2 * HALF), BF16)],
        compiler_params=params(),
        cost_estimate=pl.CostEstimate(flops=12_000_000_000, bytes_accessed=8_000_000, transcendentals=0),
        name="kept",
    )(sent.astype(F32), own_offsets, whole_grads, hidden, momentum, back_high, back_low, rows_back_high, rows_back_low)
    return (output, kept)


def solution(mesh):
    return jax.shard_map(
        on_device,
        mesh=mesh,
        in_specs=(
            P("replica", "tensor"),
            P("replica", "tensor"),
            P("replica", "tensor"),
            P(None, "tensor"),
            P(None, "tensor"),
            P("tensor", None),
            P("replica", "tensor", None),
            P(None, "tensor", None, None),
        ),
        out_specs=(P(("replica", "tensor"), None), P("replica", "tensor", None)),
        check_vma=False,
    )
```

```python
import jax
import jax.numpy as jnp
import ml_dtypes
import numpy as np
from jax import lax
from jax.experimental import pallas as pl
from jax.experimental.pallas import tpu as pltpu
from jax.sharding import PartitionSpec as P

TILE = 64
BETA_DECAY = 0.9
STEP_RATE = 0.1
PACK = 16
SPAN = 512
BAND = 256
HALF = 256
RING = 4
F32 = jnp.float32
BF16 = jnp.bfloat16


def cosine_table():
    freq = np.arange(TILE, dtype=np.float64)[:, None]
    place = np.arange(TILE, dtype=np.float64)[None, :]
    table = np.cos(np.pi * (2.0 * place + 1.0) * freq / (2.0 * TILE))
    return table * np.where(freq == 0.0, np.sqrt(1.0 / TILE), np.sqrt(2.0 / TILE))


def parts(table):
    high = table.astype(np.float32).astype(ml_dtypes.bfloat16)
    low = (table - high.astype(np.float64)).astype(np.float32).astype(ml_dtypes.bfloat16)
    return high, low


def row_table(rows):
    cosine = cosine_table()
    table = np.zeros((2 * HALF, 2 * HALF))
    for i in range(rows // TILE):
        for p in range(2):
            lanes = slice(p * HALF + i * (TILE // 2), p * HALF + (i + 1) * (TILE // 2))
            table[i * TILE : (i + 1) * TILE, lanes] = cosine[p::2].T
    return table


def band_table():
    return np.kron(np.eye(BAND // TILE), cosine_table())


def split(value):
    high = value.astype(BF16)
    return high, (value - high.astype(F32)).astype(BF16)


def dot(a, b):
    return jnp.dot(a, b, preferred_element_type=F32)


def dot_turned(a, b):
    return lax.dot_general(a, b, (((1,), (1,)), ((), ())), preferred_element_type=F32)


def momentum_spectrum_kernel(momentum, row_pair, band, out, held, twice, stack, ready, incoming, outgoing):
    steps, rows, span = held.shape

    def load(step):
        return pltpu.make_async_copy(momentum.at[0, :, pl.ds(step * span, span)], held.at[step], incoming.at[step])

    def store(step):
        return pltpu.make_async_copy(ready.at[step], out.at[pl.ds(step * span, span), :], outgoing.at[step])

    for step in range(steps):
        load(step).start()
    twice[...] = jnp.zeros_like(twice)
    bands = jnp.concatenate([band[...], band[:, :BAND]], axis=1)
    for step in range(steps):
        load(step).wait()
        turned = held[step].T
        twice[:, :rows] = turned
        twice[:, 2 * HALF : 2 * HALF + rows] = turned
        high, low = split(BETA_DECAY * dot(twice[...], row_pair[...]))
        for start in range(0, span, BAND):
            stack[:BAND] = high[start : start + BAND]
            stack[BAND : 2 * BAND] = high[start : start + BAND]
            stack[2 * BAND :] = low[start : start + BAND]
            ready[step, start : start + BAND] = dot(bands, stack[...])
        store(step).start()
    for step in range(steps):
        store(step).wait()


def weight_loads(place, gate, up, gate_held, up_held, arrived):
    width = gate.shape[1] // RING
    loads = []
    for step in range(RING):
        owner = lax.rem(place[0] + RING - step, RING)
        columns = pl.ds(pl.multiple_of(owner * width, 128), width)
        loads.append(pltpu.make_async_copy(gate.at[:, columns], gate_held.at[step], arrived.at[2 * step]))
        loads.append(pltpu.make_async_copy(up.at[:, columns], up_held.at[step], arrived.at[2 * step + 1]))
    return loads


def ring_swiglu(loads, features, gate_held, up_held):
    gated = upper = None
    for step, feature in enumerate(features):
        loads[2 * step].wait()
        term = dot(gate_held[step], feature)
        gated = term if gated is None else gated + term
        loads[2 * step + 1].wait()
        term = dot(up_held[step], feature)
        upper = term if upper is None else upper + term
    return (gated / (1.0 + jnp.exp(-gated)) * upper).astype(BF16)


def pick_kernel(place, *refs):
    pieces = refs[:RING]
    gate, up, row_pair, band, spectrum, offsets, whole_grads, hidden, own, sent = refs[RING : RING + 10]
    gate_held, up_held, spectra, grads, factor, arrived, spectra_arrived = refs[RING + 10 :]
    rows, count = hidden.shape
    width = whole_grads.shape[0] // RING
    depth = pieces[0].shape[0]
    features = width // depth
    loads = weight_loads(place, gate, up, gate_held, up_held, arrived)
    owners = [lax.rem(place[0] + RING - step, RING) for step in range(RING)]
    spectrum_loads = [
        pltpu.make_async_copy(
            spectrum.at[pl.ds(pl.multiple_of(owners[step] * width, 128), width), :],
            spectra.at[step],
            spectra_arrived.at[step],
        )
        for step in range(RING)
    ]
    for load in loads + spectrum_loads:
        load.start()
    turned = ring_swiglu(
        loads, [piece[:, :features].reshape(width, count) for piece in pieces], gate_held, up_held
    )
    hidden[...] = turned
    turned = turned.T
    high, low = split(dot(turned, row_pair[:rows]) + dot(turned, row_pair[2 * HALF : 2 * HALF + rows]))
    factor[:count] = high
    factor[count : 2 * count] = high
    factor[2 * count :] = low

    column = lax.broadcasted_iota(jnp.int32, (TILE, HALF), 0)
    for step, piece in enumerate(pieces):
        block = piece[:, features:].reshape(width, count)
        whole_grads[pl.ds(pl.multiple_of(owners[step] * width, 128), width), :] = block
        for start in range(0, width, BAND):
            size = min(BAND, width - start)
            part = block[start : start + size]
            high, low = split(dot(band[:size, :size], part) + dot(band[:size, BAND : BAND + size], part))
            grads[start : start + size, :count] = high
            grads[start : start + size, count : 2 * count] = low
            grads[start : start + size, 2 * count :] = high
        spectrum_loads[step].wait()
        total = spectra.at[step]
        total[...] += dot(grads[...], factor[...])
        for k in range(width // TILE):
            tile = owners[step] * (width // TILE) + k
            spots = offsets[place[1], pl.ds(tile, 1), :]
            even = total[k * TILE : (k + 1) * TILE, :HALF]
            odd = total[k * TILE : (k + 1) * TILE, HALF:]
            hit = jnp.where(spots == column, even, jnp.where(spots == column + TILE, odd, 0.0))
            own[pl.ds(tile, 1), :] = jnp.sum(hit, axis=0, keepdims=True)
    value = own[...].astype(BF16).astype(F32)
    own[...] = value
    packed = jnp.concatenate([value[:, : HALF // 2], value[:, HALF // 2 :]], axis=0).astype(BF16)
    for r in range(sent.shape[0]):
        sent[r] = packed


def next_kernel(place, *refs):
    pieces = refs[:RING]
    gate, up, down, row_pair, base, factor = refs[RING : RING + 6]
    gate_held, up_held, down_held, arrived, down_arrived = refs[RING + 6 :]
    count = base.shape[0]
    rows = down.shape[0]
    loads = weight_loads(place, gate, up, gate_held, up_held, arrived)
    down_load = pltpu.make_async_copy(down, down_held, down_arrived.at[0])
    for load in loads:
        load.start()
    down_load.start()
    features = []
    for piece in pieces:
        value = piece[...].astype(F32)
        blocks = []
        for d in range(value.shape[0]):
            blocks += [value[d, :, :count], value[d, :, count:]]
        features.append(jnp.concatenate(blocks, axis=0).astype(BF16))
    turned = ring_swiglu(loads, features, gate_held, up_held).T
    along = (dot(turned, row_pair[:rows]) + dot(turned, row_pair[2 * HALF : 2 * HALF + rows])).T
    factor[...] = jnp.concatenate(split(along), axis=1)
    down_load.wait()
    base[...] = dot(turned, down_held[...])


def output_kernel(values, offsets, next_rows, base, back, out, dense, across, rearranged, columns, even_values, odd_values):
    replicas, tile_cols, _ = offsets.shape
    tokens = base.shape[0]
    bands = base.shape[1] // BAND
    chunks = base.shape[1] // 128
    for r in range(replicas):
        value = values[r].astype(F32)
        value = jnp.concatenate([value[:tile_cols], value[tile_cols:]], axis=1)
        columns[r] = (offsets[r] & (TILE - 1)).astype(F32)
        even_values[r] = jnp.where(offsets[r] < TILE, value, 0.0)
        odd_values[r] = jnp.where(offsets[r] < TILE, 0.0, value)
    place = lax.broadcasted_iota(jnp.int32, (TILE, 128), 0).astype(F32).astype(BF16)
    zero = jnp.zeros((PACK, 128), BF16)

    def one(tile, carry):
        for start in range(0, HALF, 128):
            listed = []
            for r in range(replicas):
                rows = (table[r, pl.ds(tile, 1), :][:, start : start + 128] for table in (columns, even_values, odd_values))
                listed.append([jnp.broadcast_to(row, (PACK, 128)).astype(BF16) for row in rows])
            for first in range(0, TILE, PACK):
                even, odd = zero, zero
                for spots, even_value, odd_value in listed:
                    hit = spots == place[first : first + PACK]
                    even += jnp.where(hit, even_value, zero)
                    odd += jnp.where(hit, odd_value, zero)
                row = pl.ds(pl.multiple_of(tile * TILE + first, PACK), PACK)
                dense[row, start : start + 128] = even
                dense[row, HALF + start : HALF + start + 128] = odd
        return carry

    lax.fori_loop(0, tile_cols, one, 0)
    for step in range(0, bands, 2):
        both = dot(dense[step * BAND : (step + 2) * BAND], next_rows[...]).astype(BF16)
        for k in range(2):
            part = both[k * BAND : (k + 1) * BAND]
            across[:BAND, (step + k) * 128 : (step + k + 1) * 128] = part
            across[BAND:, (step + k) * 128 : (step + k + 1) * 128] = part
    change = dot(back[...], across[...])
    for step in range(bands):
        turned = change[:, step * 128 : (step + 1) * 128].T
        result = base[:, step * BAND : (step + 1) * BAND] - (STEP_RATE / replicas) * (turned[:tokens] + turned[tokens:])
        for c in range(BAND // 128):
            rearranged[pl.ds(step * (BAND // 128) + c, tokens, stride=chunks), :] = result[:, c * 128 : (c + 1) * 128]
    out[...] = rearranged[...].astype(BF16)


def kept_kernel(
    place, own, offsets, cotangent, hidden, momentum, row_pair, back, out, held, ready, dense, left, right, incoming, outgoing
):
    steps, rows, span = held.shape
    spectral = 2 * HALF

    def load(step):
        return pltpu.make_async_copy(momentum.at[0, :, pl.ds(step * span, span)], held.at[step], incoming.at[step])

    def store(step):
        return pltpu.make_async_copy(ready.at[step], out.at[0, :, pl.ds(step * span, span)], outgoing.at[step])

    for step in range(steps):
        load(step).start()
    left[:, :spectral] = row_pair[:rows]
    left[:, spectral : 2 * spectral] = row_pair[:rows]
    left[:, 2 * spectral : 3 * spectral] = row_pair[spectral : spectral + rows]
    left[:, 3 * spectral :] = -hidden[...]
    column = lax.broadcasted_iota(jnp.int32, (TILE, HALF), 0)
    for step in range(steps):
        for start in range(0, span, BAND):
            for k in range(BAND // TILE):
                tile = (step * span + start) // TILE + k
                spots, value = offsets[place[1], tile : tile + 1, :], own[tile : tile + 1, :]
                even = jnp.where(spots == column, value, 0.0).astype(BF16)
                odd = jnp.where(spots == column + TILE, value, 0.0).astype(BF16)
                for copy in range(2):
                    dense[copy * BAND + k * TILE : copy * BAND + (k + 1) * TILE, :HALF] = even
                    dense[copy * BAND + k * TILE : copy * BAND + (k + 1) * TILE, HALF:] = odd
            high, low = split(dot(back[...], dense[...]))
            right[start : start + BAND, :spectral] = high
            right[start : start + BAND, spectral : 2 * spectral] = low
            right[start : start + BAND, 2 * spectral : 3 * spectral] = high
        right[:, 3 * spectral :] = cotangent[step * span : (step + 1) * span]
        change = dot_turned(left[...], right[...])
        load(step).wait()
        ready[step] = (BETA_DECAY * held[step].astype(F32) - change).astype(BF16)
        store(step).start()
    for step in range(steps):
        store(step).wait()


IN_VMEM = pl.BlockSpec(memory_space=pltpu.VMEM)
IN_SMEM = pl.BlockSpec(memory_space=pltpu.SMEM)
IN_HBM = pl.BlockSpec(memory_space=pltpu.HBM)


def params(limit=58):
    return pltpu.CompilerParams(vmem_limit_bytes=limit * 1024 * 1024)


def cost(flops, moved):
    return pl.CostEstimate(flops=int(flops), bytes_accessed=int(moved), transcendentals=0)


def depth_gather(block, depth):
    groups = [[x * depth + z for z in range(depth)] for x in range(RING)]
    blocks = jnp.broadcast_to(block[None], (depth,) + block.shape)
    return lax.all_to_all(blocks, "tensor", 0, 0, tiled=True, axis_index_groups=groups)


def ring_gather(block, depth):
    pieces = [block]
    for step in range(1, RING):
        pairs = [(x * depth + z, (x + step) % RING * depth + z) for x in range(RING) for z in range(depth)]
        pieces.append(lax.ppermute(block, "tensor", pairs))
    return pieces


def on_device(tokens, next_tokens, cotangent, gate_weight, up_weight, down_weight, momentum, indices):
    shards = lax.axis_size("tensor")
    depth = shards // RING
    replicas = lax.axis_size("replica")
    place = jnp.stack([lax.axis_index("tensor") // depth, lax.axis_index("replica")]).astype(jnp.int32)
    rows, width = down_weight.shape
    bands = width // BAND
    part = width // RING
    tile_rows, tile_cols, keep = indices.shape[1:]
    stride = TILE * TILE // keep
    count, next_count, features = tokens.shape[0], next_tokens.shape[0], tokens.shape[1]
    row_pair = jnp.asarray(np.concatenate(parts(row_table(rows))))
    band = jnp.asarray(np.concatenate(parts(band_table()), axis=1))
    back = jnp.asarray(np.concatenate(parts(band_table().T), axis=1))
    gate, up = gate_weight.T, up_weight.T

    turned = next_tokens.T
    packed = jnp.concatenate([turned[: features // 2], turned[features // 2 :]], axis=1)
    gathered = depth_gather(jnp.concatenate([tokens.T, cotangent.T, packed]), depth)
    pieces = ring_gather(gathered[:, : 2 * features], depth)
    nexts = ring_gather(gathered[:, 2 * features :], depth)

    offsets = indices - jnp.arange(keep, dtype=jnp.int32) * stride
    offsets = offsets.transpose(0, 2, 1, 3).reshape(replicas, tile_cols, tile_rows * keep)
    offsets = jnp.pad(offsets, ((0, 0), (0, 0), (0, HALF - tile_rows * keep)), constant_values=-1)

    def shape(dims, kind):
        return jax.ShapeDtypeStruct(dims, kind)

    dma = pltpu.SemaphoreType.DMA
    weights_held = [pltpu.VMEM((RING, rows, part), BF16)] * 2

    spectrum = pl.pallas_call(
        momentum_spectrum_kernel,
        in_specs=[IN_HBM, IN_VMEM, IN_VMEM],
        out_specs=IN_HBM,
        out_shape=shape((width, 2 * HALF), F32),
        scratch_shapes=[
            pltpu.VMEM((width // SPAN, rows, SPAN), BF16),
            pltpu.VMEM((SPAN, 4 * HALF), BF16),
            pltpu.VMEM((3 * BAND, 2 * HALF), BF16),
            pltpu.VMEM((width // SPAN, SPAN, 2 * HALF), F32),
            dma((width // SPAN,)),
            dma((width // SPAN,)),
        ],
        compiler_params=params(),
        cost_estimate=cost(6e9, 8e6),
        name="momentum_spectrum",
    )(momentum, row_pair, band)

    whole_grads, hidden, own, sent = pl.pallas_call(
        pick_kernel,
        in_specs=[IN_SMEM] + [IN_VMEM] * RING + [IN_HBM] * 2 + [IN_VMEM] * 2 + [IN_HBM, IN_VMEM],
        out_specs=[IN_VMEM] * 4,
        out_shape=[
            shape((width, count), BF16),
            shape((rows, count), BF16),
            shape((tile_cols, HALF), F32),
            shape((replicas, 2 * tile_cols, HALF // 2), BF16),
        ],
        scratch_shapes=weights_held
        + [
            pltpu.VMEM((RING, part, 2 * HALF), F32),
            pltpu.VMEM((part, 3 * count), BF16),
            pltpu.VMEM((3 * count, 2 * HALF), BF16),
            dma((2 * RING,)),
            dma((RING,)),
        ],
        compiler_params=params(),
        cost_estimate=cost(6e9, 12e6),
        name="pick",
    )(place, *pieces, gate, up, row_pair, band, spectrum, offsets)

    listed = lax.all_to_all(sent, "replica", 0, 0, tiled=True)

    base, next_rows = pl.pallas_call(
        next_kernel,
        in_specs=[IN_SMEM] + [IN_VMEM] * RING + [IN_HBM] * 3 + [IN_VMEM],
        out_specs=[IN_VMEM] * 2,
        out_shape=[shape((next_count, width), F32), shape((2 * HALF, 2 * next_count), BF16)],
        scratch_shapes=weights_held + [pltpu.VMEM((rows, width), BF16), dma((2 * RING,)), dma((1,))],
        compiler_params=params(),
        cost_estimate=cost(2e9, 7e6),
        name="next_hidden",
    )(place, *nexts, gate, up, down_weight, row_pair)

    partial = pl.pallas_call(
        output_kernel,
        in_specs=[IN_VMEM] * 5,
        out_specs=IN_VMEM,
        out_shape=shape((next_count * width // 128, 128), BF16),
        scratch_shapes=[
            pltpu.VMEM((width, 2 * HALF), BF16),
            pltpu.VMEM((2 * BAND, bands * 2 * next_count), BF16),
            pltpu.VMEM((next_count * width // 128, 128), F32),
        ]
        + [pltpu.VMEM((replicas, tile_cols, HALF), F32)] * 3,
        compiler_params=params(),
        cost_estimate=cost(4e9, 4e6),
        name="output_part",
    )(listed, offsets, next_rows, base, back)

    received = lax.all_to_all(partial.reshape(shards, -1, 128), "tensor", 0, 0, tiled=True)
    output = jnp.sum(received.astype(F32), axis=0).astype(BF16).reshape(next_count // shards, width)

    kept = pl.pallas_call(
        kept_kernel,
        in_specs=[IN_SMEM] + [IN_VMEM] * 4 + [IN_HBM, IN_VMEM, IN_VMEM],
        out_specs=IN_HBM,
        out_shape=shape((1, rows, width), BF16),
        scratch_shapes=[pltpu.VMEM((width // SPAN, rows, SPAN), BF16)] * 2
        + [
            pltpu.VMEM((2 * BAND, 2 * HALF), BF16),
            pltpu.VMEM((rows, 6 * HALF + count), BF16),
            pltpu.VMEM((SPAN, 6 * HALF + count), BF16),
            dma((width // SPAN,)),
            dma((width // SPAN,)),
        ],
        compiler_params=params(),
        cost_estimate=cost(10e9, 8e6),
        name="kept",
    )(place, own, offsets, whole_grads, hidden, momentum, row_pair, back)
    return (output, kept)


def solution(mesh):
    return jax.shard_map(
        on_device,
        mesh=mesh,
        in_specs=(
            P("replica", "tensor"),
            P("replica", "tensor"),
            P("replica", "tensor"),
            P(None, "tensor"),
            P(None, "tensor"),
            P("tensor", None),
            P("replica", "tensor", None),
            P(None, "tensor", None, None),
        ),
        out_specs=(P(("replica", "tensor"), None), P("replica", "tensor", None)),
        check_vma=False,
    )
```

```python
import jax
import jax.numpy as jnp
import ml_dtypes
import numpy as np
from jax import lax
from jax.experimental import pallas as pl
from jax.experimental.pallas import tpu as pltpu
from jax.sharding import PartitionSpec as P

TILE = 64
BETA_DECAY = 0.9
STEP_RATE = 0.1
ROOM = 32 << 20
PACK = 16
SPAN = 512
BAND = 256
HALF = 256
RING = 4
F32 = jnp.float32
BF16 = jnp.bfloat16


def cosine_table():
    freq = np.arange(TILE, dtype=np.float64)[:, None]
    place = np.arange(TILE, dtype=np.float64)[None, :]
    table = np.cos(np.pi * (2.0 * place + 1.0) * freq / (2.0 * TILE))
    return table * np.where(freq == 0.0, np.sqrt(1.0 / TILE), np.sqrt(2.0 / TILE))


def parts(table):
    high = table.astype(np.float32).astype(ml_dtypes.bfloat16)
    low = (table - high.astype(np.float64)).astype(np.float32).astype(ml_dtypes.bfloat16)
    return high, low


def row_table(rows):
    cosine = cosine_table()
    table = np.zeros((2 * HALF, 2 * HALF))
    for i in range(rows // TILE):
        for p in range(2):
            lanes = slice(p * HALF + i * (TILE // 2), p * HALF + (i + 1) * (TILE // 2))
            table[i * TILE : (i + 1) * TILE, lanes] = cosine[p::2].T
    return table


def band_table():
    return np.kron(np.eye(BAND // TILE), cosine_table())


def split(value):
    high = value.astype(BF16)
    return high, (value - high.astype(F32)).astype(BF16)


def dot(a, b):
    return jnp.dot(a, b, preferred_element_type=F32)


def dot_turned(a, b):
    return lax.dot_general(a, b, (((1,), (1,)), ((), ())), preferred_element_type=F32)


def pack_kernel(tokens, cotangent, next_tokens, out):
    features, count = tokens.shape
    turned = next_tokens[...].astype(F32).T
    packed = jnp.concatenate([turned[: features // 2], turned[features // 2 :]], axis=1).astype(BF16)
    for d in range(out.shape[0]):
        out[d, :features] = tokens[...]
        out[d, features : 2 * features] = cotangent[...]
        out[d, 2 * features :] = packed


def picked(total, spots):
    column = lax.broadcasted_iota(jnp.int32, (TILE, HALF), 0)
    hit = jnp.where(spots == column, total[:, :HALF], jnp.where(spots == column + TILE, total[:, HALF:], 0.0))
    return jnp.sum(hit, axis=0, keepdims=True)


def momentum_pick_kernel(
    place, momentum, gate, up, row_pair, band, offsets, out, gate_held, up_held, held, twice, stack, incoming, arrived
):
    steps, rows, span = held.shape

    def load(step):
        return pltpu.make_async_copy(momentum.at[0, :, pl.ds(step * span, span)], held.at[step], incoming.at[step])

    for step in range(steps):
        load(step).start()
    weights = weight_loads(place, gate, up, gate_held, up_held, arrived)
    for weight in weights:
        weight.start()
    twice[...] = jnp.zeros_like(twice)
    bands = jnp.concatenate([band[...], band[:, :BAND]], axis=1)
    for step in range(steps):
        load(step).wait()
        turned = held[step].T
        twice[:, :rows] = turned
        twice[:, 2 * HALF : 2 * HALF + rows] = turned
        high, low = split(BETA_DECAY * dot(twice[...], row_pair[...]))
        for start in range(0, span, BAND):
            stack[:BAND] = high[start : start + BAND]
            stack[BAND : 2 * BAND] = high[start : start + BAND]
            stack[2 * BAND :] = low[start : start + BAND]
            total = dot(bands, stack[...])
            for k in range(BAND // TILE):
                tile = (step * span + start) // TILE + k
                spots = offsets[place[1], tile : tile + 1, :]
                out[tile : tile + 1, :] = picked(total[k * TILE : (k + 1) * TILE], spots)
    for weight in weights:
        weight.wait()


def weight_loads(place, gate, up, gate_held, up_held, arrived):
    width = gate.shape[1] // RING
    loads = []
    for step in range(RING):
        owner = lax.rem(place[0] + RING - step, RING)
        columns = pl.ds(pl.multiple_of(owner * width, 128), width)
        loads.append(pltpu.make_async_copy(gate.at[:, columns], gate_held.at[step], arrived.at[2 * step]))
        loads.append(pltpu.make_async_copy(up.at[:, columns], up_held.at[step], arrived.at[2 * step + 1]))
    return loads


def ring_swiglu(features, gate_held, up_held):
    gated = upper = None
    for step, feature in enumerate(features):
        term = dot(gate_held[step], feature)
        gated = term if gated is None else gated + term
        term = dot(up_held[step], feature)
        upper = term if upper is None else upper + term
    return (gated / (1.0 + jnp.exp(-gated)) * upper).astype(BF16)


def pick_kernel(place, *refs):
    pieces = refs[:RING]
    gate_held, up_held, row_pair, band, momentum_part, offsets = refs[RING : RING + 6]
    whole_grads, hidden, next_hidden, sent = refs[RING + 6 : RING + 10]
    grads, total, factor, rows_held, units, next_units, coefficients, packed_held, rows_arrived, left = refs[RING + 10 :]
    rows, count = hidden.shape
    next_count = next_hidden.shape[1]
    depth, features = pieces[0].shape[0], whole_grads.shape[1]
    width = depth * features
    owners = [lax.rem(place[0] + RING - step, RING) for step in range(RING)]
    rows_load = pltpu.make_async_copy(row_pair, rows_held, rows_arrived.at[0])
    rows_load.start()
    stores = [
        pltpu.make_async_copy(
            piece.at[:, features : 2 * features], whole_grads.at[pl.ds(owners[step] * depth, depth)], left.at[step]
        )
        for step, piece in enumerate(pieces)
    ]
    for store in stores:
        store.start()

    for step, piece in enumerate(pieces):
        block = piece[:, features : 2 * features].reshape(width, count)
        for start in range(0, width, BAND):
            size = min(BAND, width - start)
            part = block[start : start + size]
            high, low = split(dot(band[:size, :size], part) + dot(band[:size, BAND : BAND + size], part))
            row = slice(step * width + start, step * width + start + size)
            grads[row, :count] = high
            grads[row, count : 2 * count] = low
            grads[row, 2 * count :] = high

    feature_blocks = []
    for piece in pieces:
        packed = piece[:, 2 * features :].astype(F32)
        blocks = []
        for d in range(depth):
            blocks += [packed[d, :, :next_count], packed[d, :, next_count:]]
        nexts = jnp.concatenate(blocks, axis=0).astype(BF16)
        feature_blocks.append(jnp.concatenate([piece[:, :features].reshape(width, count), nexts], axis=1))
    turned = ring_swiglu(feature_blocks, gate_held, up_held)
    units[...] = turned[:, :count]
    next_units[...] = turned[:, count:]
    for source, target in ((units, hidden), (next_units, next_hidden)):
        stores.append(pltpu.make_async_copy(source, target, left.at[len(stores)]))
        stores[-1].start()
    turned = turned[:, :count].T
    rows_load.wait()
    high, low = split(dot(turned, rows_held[:rows]) + dot(turned, rows_held[2 * HALF : 2 * HALF + rows]))
    factor[:count] = high
    factor[count : 2 * count] = high
    factor[2 * count :] = low

    for step in range(RING):
        total[...] = dot(grads[step * width : (step + 1) * width], factor[...])
        for k in range(width // TILE):
            tile = owners[step] * (width // TILE) + k
            row = pl.ds(tile, 1)
            spots = offsets[place[1], row, :]
            coefficients[row, :] = picked(total[k * TILE : (k + 1) * TILE], spots) + momentum_part[row, :]
    value = coefficients[...]
    packed_held[...] = jnp.concatenate([value[:, : HALF // 2], value[:, HALF // 2 :]], axis=0).astype(BF16)
    for target in [sent.at[r] for r in range(sent.shape[0])]:
        stores.append(pltpu.make_async_copy(packed_held, target, left.at[len(stores)]))
        stores[-1].start()
    for store in stores:
        store.wait()


def next_kernel(next_hidden, down, row_pair, base, factor, down_held, base_held, down_arrived, base_left):
    rows = down.shape[0]
    bands = down_held.shape[0]
    span = down_held.shape[2]
    loads = [
        pltpu.make_async_copy(down.at[:, pl.ds(step * span, span)], down_held.at[step], down_arrived.at[step])
        for step in range(bands)
    ]
    for load in loads:
        load.start()
    turned = next_hidden[...].T
    along = (dot(turned, row_pair[:rows]) + dot(turned, row_pair[2 * HALF : 2 * HALF + rows])).T
    factor[...] = jnp.concatenate(split(along), axis=1)
    for step, load in enumerate(loads):
        load.wait()
        base_held[:, step * span : (step + 1) * span] = dot(turned, down_held[step])
    store = pltpu.make_async_copy(base_held, base.at[: turned.shape[0]], base_left.at[0])
    store.start()
    store.wait()


def output_kernel(
    values, offsets, next_rows, base_whole, back, out,
    base, dense, across, rearranged, columns, even_values, odd_values, base_arrived,
):
    replicas, tile_cols, _ = offsets.shape
    tokens = base.shape[0]
    base_load = pltpu.make_async_copy(base_whole.at[:tokens], base, base_arrived.at[0])
    base_load.start()
    bands = base.shape[1] // BAND
    chunks = base.shape[1] // 128
    for r in range(replicas):
        value = values[r].astype(F32)
        value = jnp.concatenate([value[:tile_cols], value[tile_cols:]], axis=1)
        columns[r] = (offsets[r] & (TILE - 1)).astype(F32)
        even_values[r] = jnp.where(offsets[r] < TILE, value, 0.0)
        odd_values[r] = jnp.where(offsets[r] < TILE, 0.0, value)
    place = lax.broadcasted_iota(jnp.int32, (TILE, 128), 0).astype(F32).astype(BF16)
    zero = jnp.zeros((PACK, 128), BF16)

    def one(tile, carry):
        for start in range(0, HALF, 128):
            listed = []
            for r in range(replicas):
                rows = (table[r, pl.ds(tile, 1), :][:, start : start + 128] for table in (columns, even_values, odd_values))
                listed.append([jnp.broadcast_to(row, (PACK, 128)).astype(BF16) for row in rows])
            for first in range(0, TILE, PACK):
                even, odd = zero, zero
                for spots, even_value, odd_value in listed:
                    hit = spots == place[first : first + PACK]
                    even += jnp.where(hit, even_value, zero)
                    odd += jnp.where(hit, odd_value, zero)
                row = pl.ds(pl.multiple_of(tile * TILE + first, PACK), PACK)
                dense[row, start : start + 128] = even
                dense[row, HALF + start : HALF + start + 128] = odd
        return carry

    lax.fori_loop(0, tile_cols, one, 0)
    for step in range(0, bands, 2):
        both = dot(dense[step * BAND : (step + 2) * BAND], next_rows[...]).astype(BF16)
        for k in range(2):
            part = both[k * BAND : (k + 1) * BAND]
            across[:BAND, (step + k) * 128 : (step + k + 1) * 128] = part
            across[BAND:, (step + k) * 128 : (step + k + 1) * 128] = part
    change = dot(back[...], across[...])
    base_load.wait()
    for step in range(bands):
        turned = change[:, step * 128 : (step + 1) * 128].T
        result = base[:, step * BAND : (step + 1) * BAND] - (STEP_RATE / replicas) * (turned[:tokens] + turned[tokens:])
        for c in range(BAND // 128):
            rearranged[pl.ds(step * (BAND // 128) + c, tokens, stride=chunks), :] = result[:, c * 128 : (c + 1) * 128]
    out[...] = rearranged[...].astype(BF16)


def kept_kernel(
    place, sent, offsets, whole_grads, hidden, momentum, row_pair, back, out,
    own, cotangent, held, ready, dense, left, right, incoming, outgoing, grads_arrived,
):
    steps, rows, span = held.shape
    spectral = 2 * HALF

    def load(step):
        return pltpu.make_async_copy(momentum.at[0, :, pl.ds(step * span, span)], held.at[step], incoming.at[step])

    def store(step):
        return pltpu.make_async_copy(ready.at[step], out.at[0, :, pl.ds(step * span, span)], outgoing.at[step])

    grads_load = pltpu.make_async_copy(whole_grads.at[: cotangent.shape[0]], cotangent, grads_arrived.at[0])
    grads_load.start()
    for step in range(steps):
        load(step).start()
    value = sent[0].astype(F32)
    own[...] = jnp.concatenate([value[: own.shape[0]], value[own.shape[0] :]], axis=1)
    left[:, :spectral] = row_pair[:rows]
    left[:, spectral : 2 * spectral] = row_pair[:rows]
    left[:, 2 * spectral : 3 * spectral] = row_pair[spectral : spectral + rows]
    left[:, 3 * spectral :] = -hidden[...]
    column = lax.broadcasted_iota(jnp.int32, (TILE, HALF), 0)
    grads_load.wait()
    grads = cotangent[...].reshape(steps * span, cotangent.shape[2])
    for step in range(steps):
        for start in range(0, span, BAND):
            for k in range(BAND // TILE):
                tile = (step * span + start) // TILE + k
                spots, value = offsets[place[1], tile : tile + 1, :], own[tile : tile + 1, :]
                even = jnp.where(spots == column, value, 0.0).astype(BF16)
                odd = jnp.where(spots == column + TILE, value, 0.0).astype(BF16)
                for copy in range(2):
                    dense[copy * BAND + k * TILE : copy * BAND + (k + 1) * TILE, :HALF] = even
                    dense[copy * BAND + k * TILE : copy * BAND + (k + 1) * TILE, HALF:] = odd
            high, low = split(dot(back[...], dense[...]))
            right[start : start + BAND, :spectral] = high
            right[start : start + BAND, spectral : 2 * spectral] = low
            right[start : start + BAND, 2 * spectral : 3 * spectral] = high
        right[:, 3 * spectral :] = grads[step * span : (step + 1) * span]
        change = dot_turned(left[...], right[...])
        load(step).wait()
        ready[step] = (BETA_DECAY * held[step].astype(F32) - change).astype(BF16)
        store(step).start()
    for step in range(steps):
        store(step).wait()


def sum_kernel(received, out):
    total = jnp.sum(received[...].astype(F32), axis=0)
    chunks = out.shape[1] // 128
    lines = [
        jnp.concatenate([total[h * chunks + c : h * chunks + c + 1] for c in range(chunks)], axis=1)
        for h in range(out.shape[0])
    ]
    out[...] = jnp.concatenate(lines, axis=0).astype(BF16)


IN_VMEM = pl.BlockSpec(memory_space=pltpu.VMEM)
IN_SMEM = pl.BlockSpec(memory_space=pltpu.SMEM)
IN_HBM = pl.BlockSpec(memory_space=pltpu.HBM)


def params(limit=36):
    return pltpu.CompilerParams(vmem_limit_bytes=limit * 1024 * 1024)


def cost(flops, moved):
    return pl.CostEstimate(flops=int(flops), bytes_accessed=int(moved), transcendentals=0)


def depth_gather(block, depth):
    groups = [[x * depth + z for z in range(depth)] for x in range(RING)]
    return lax.all_to_all(block, "tensor", 0, 0, tiled=True, axis_index_groups=groups)


def ring_gather(block, depth):
    pieces = [block]
    for step in range(1, RING):
        pairs = [(x * depth + z, (x + step) % RING * depth + z) for x in range(RING) for z in range(depth)]
        pieces.append(lax.ppermute(block, "tensor", pairs))
    return pieces


def on_device(tokens, next_tokens, cotangent, gate_weight, up_weight, down_weight, momentum, indices):
    shards = lax.axis_size("tensor")
    depth = shards // RING
    replicas = lax.axis_size("replica")
    place = jnp.stack([lax.axis_index("tensor") // depth, lax.axis_index("replica")]).astype(jnp.int32)
    rows, width = down_weight.shape
    bands = width // BAND
    part = width // RING
    tile_rows, tile_cols, keep = indices.shape[1:]
    stride = TILE * TILE // keep
    count, next_count, features = tokens.shape[0], next_tokens.shape[0], tokens.shape[1]
    row_pair = jnp.asarray(np.concatenate(parts(row_table(rows))))
    band = jnp.asarray(np.concatenate(parts(band_table()), axis=1))
    back = jnp.asarray(np.concatenate(parts(band_table().T), axis=1))
    gate, up = gate_weight.T, up_weight.T

    packed = pl.pallas_call(
        pack_kernel,
        in_specs=[IN_VMEM] * 3,
        out_specs=IN_VMEM,
        out_shape=jax.ShapeDtypeStruct((depth, 2 * features + features // 2, count), BF16),
        compiler_params=params(58),
        name="pack",
    )(tokens.T, cotangent.T, next_tokens)
    pieces = ring_gather(depth_gather(packed, depth), depth)

    offsets = indices - jnp.arange(keep, dtype=jnp.int32) * stride
    offsets = offsets.transpose(0, 2, 1, 3).reshape(replicas, tile_cols, tile_rows * keep)
    offsets = jnp.pad(offsets, ((0, 0), (0, 0), (0, HALF - tile_rows * keep)), constant_values=-1)

    def shape(dims, kind):
        return jax.ShapeDtypeStruct(dims, kind)

    dma = pltpu.SemaphoreType.DMA

    momentum_part, gate_held, up_held = pl.pallas_call(
        momentum_pick_kernel,
        in_specs=[IN_SMEM] + [IN_HBM] * 3 + [IN_VMEM] * 3,
        out_specs=[IN_VMEM] * 3,
        out_shape=[shape((tile_cols, HALF), F32)] + [shape((RING, rows, part), BF16)] * 2,
        scratch_shapes=[
            pltpu.VMEM((width // SPAN, rows, SPAN), BF16),
            pltpu.VMEM((SPAN, 4 * HALF), BF16),
            pltpu.VMEM((3 * BAND, 2 * HALF), BF16),
            dma((width // SPAN,)),
            dma((2 * RING,)),
        ],
        compiler_params=params(36),
        cost_estimate=cost(6e9, 8e6),
        name="momentum_pick",
    )(place, momentum, gate, up, row_pair, band, offsets)

    whole_grads, hidden, next_hidden, sent = pl.pallas_call(
        pick_kernel,
        in_specs=[IN_SMEM] + [IN_VMEM] * (RING + 2) + [IN_HBM] + [IN_VMEM] * 3,
        out_specs=[IN_HBM] * 4,
        out_shape=[
            shape((ROOM // (features * count * 2), features, count), BF16),
            shape((rows, count), BF16),
            shape((rows, next_count), BF16),
            shape((replicas, 2 * tile_cols, HALF // 2), BF16),
        ],
        scratch_shapes=[
            pltpu.VMEM((width, 3 * count), BF16),
            pltpu.VMEM((part, 2 * HALF), F32),
            pltpu.VMEM((3 * count, 2 * HALF), BF16),
            pltpu.VMEM((4 * HALF, 2 * HALF), BF16),
            pltpu.VMEM((rows, count), BF16),
            pltpu.VMEM((rows, next_count), BF16),
            pltpu.VMEM((tile_cols, HALF), F32),
            pltpu.VMEM((2 * tile_cols, HALF // 2), BF16),
            dma((1,)),
            dma((RING + 2 + replicas,)),
        ],
        compiler_params=params(36),
        cost_estimate=cost(6e9, 12e6),
        name="pick",
    )(place, *pieces, gate_held, up_held, row_pair, band, momentum_part, offsets)

    listed = lax.all_to_all(sent, "replica", 0, 0, tiled=True)

    base, next_rows = pl.pallas_call(
        next_kernel,
        in_specs=[IN_VMEM, IN_HBM, IN_VMEM],
        out_specs=[IN_HBM, IN_VMEM],
        out_shape=[shape((ROOM // (width * 4), width), F32), shape((2 * HALF, 2 * next_count), BF16)],
        scratch_shapes=[
            pltpu.VMEM((width // SPAN, rows, SPAN), BF16),
            pltpu.VMEM((next_count, width), F32),
            dma((width // SPAN,)),
            dma((1,)),
        ],
        compiler_params=params(),
        cost_estimate=cost(2e9, 7e6),
        name="next_rows",
    )(next_hidden, down_weight, row_pair)

    partial = pl.pallas_call(
        output_kernel,
        in_specs=[IN_VMEM] * 3 + [IN_HBM, IN_VMEM],
        out_specs=IN_VMEM,
        out_shape=shape((next_count * width // 128, 128), BF16),
        scratch_shapes=[
            pltpu.VMEM((next_count, width), F32),
            pltpu.VMEM((width, 2 * HALF), BF16),
            pltpu.VMEM((2 * BAND, bands * 2 * next_count), BF16),
            pltpu.VMEM((next_count * width // 128, 128), F32),
        ]
        + [pltpu.VMEM((replicas, tile_cols, HALF), F32)] * 3
        + [dma((1,))],
        compiler_params=params(),
        cost_estimate=cost(4e9, 4e6),
        name="output_part",
    )(listed, offsets, next_rows, base, back)

    received = lax.all_to_all(partial.reshape(shards, -1, 128), "tensor", 0, 0, tiled=True)
    output = pl.pallas_call(
        sum_kernel,
        in_specs=[IN_VMEM],
        out_specs=IN_VMEM,
        out_shape=shape((next_count // shards, width), BF16),
        compiler_params=params(),
        name="output_sum",
    )(received)

    kept = pl.pallas_call(
        kept_kernel,
        in_specs=[IN_SMEM, IN_VMEM, IN_VMEM, IN_HBM, IN_VMEM, IN_HBM, IN_VMEM, IN_VMEM],
        out_specs=IN_HBM,
        out_shape=shape((1, rows, width), BF16),
        scratch_shapes=[pltpu.VMEM((tile_cols, HALF), F32), pltpu.VMEM((shards, features, count), BF16)]
        + [pltpu.VMEM((width // SPAN, rows, SPAN), BF16)] * 2
        + [
            pltpu.VMEM((2 * BAND, 2 * HALF), BF16),
            pltpu.VMEM((rows, 6 * HALF + count), BF16),
            pltpu.VMEM((SPAN, 6 * HALF + count), BF16),
            dma((width // SPAN,)),
            dma((width // SPAN,)),
            dma((1,)),
        ],
        compiler_params=params(),
        cost_estimate=cost(10e9, 8e6),
        name="kept",
    )(place, sent, offsets, whole_grads, hidden, momentum, row_pair, back)
    return (output, kept)


def solution(mesh):
    return jax.shard_map(
        on_device,
        mesh=mesh,
        in_specs=(
            P("replica", "tensor"),
            P("replica", "tensor"),
            P("replica", "tensor"),
            P(None, "tensor"),
            P(None, "tensor"),
            P("tensor", None),
            P("replica", "tensor", None),
            P(None, "tensor", None, None),
        ),
        out_specs=(P(("replica", "tensor"), None), P("replica", "tensor", None)),
        check_vma=False,
    )
```

```python
import jax
import jax.numpy as jnp
import ml_dtypes
import numpy as np
from jax import lax
from jax.experimental import pallas as pl
from jax.experimental.pallas import tpu as pltpu
from jax.sharding import PartitionSpec as P

TILE = 64
BETA_DECAY = 0.9
STEP_RATE = 0.1
ROOM = 32 << 20
PACK = 16
SPAN = 512
BAND = 256
HALF = 256
RING = 4
F32 = jnp.float32
BF16 = jnp.bfloat16


def cosine_table():
    freq = np.arange(TILE, dtype=np.float64)[:, None]
    place = np.arange(TILE, dtype=np.float64)[None, :]
    table = np.cos(np.pi * (2.0 * place + 1.0) * freq / (2.0 * TILE))
    return table * np.where(freq == 0.0, np.sqrt(1.0 / TILE), np.sqrt(2.0 / TILE))


def parts(table):
    high = table.astype(np.float32).astype(ml_dtypes.bfloat16)
    low = (table - high.astype(np.float64)).astype(np.float32).astype(ml_dtypes.bfloat16)
    return high, low


def row_table(rows):
    cosine = cosine_table()
    table = np.zeros((2 * HALF, 2 * HALF))
    for i in range(rows // TILE):
        for p in range(2):
            lanes = slice(p * HALF + i * (TILE // 2), p * HALF + (i + 1) * (TILE // 2))
            table[i * TILE : (i + 1) * TILE, lanes] = cosine[p::2].T
    return table


def band_table():
    return np.kron(np.eye(BAND // TILE), cosine_table())


def split(value):
    high = value.astype(BF16)
    return high, (value - high.astype(F32)).astype(BF16)


def dot(a, b):
    return jnp.dot(a, b, preferred_element_type=F32)


def dot_turned(a, b):
    return lax.dot_general(a, b, (((1,), (1,)), ((), ())), preferred_element_type=F32)


def pack_kernel(tokens, cotangent, next_tokens, out):
    features, count = tokens.shape
    turned = next_tokens[...].astype(F32).T
    packed = jnp.concatenate([turned[: features // 2], turned[features // 2 :]], axis=1).astype(BF16)
    for d in range(out.shape[0]):
        out[d, :features] = tokens[...]
        out[d, features : 2 * features] = cotangent[...]
        out[d, 2 * features :] = packed


def picked(total, spots):
    column = lax.broadcasted_iota(jnp.int32, (TILE, HALF), 0)
    hit = jnp.where(spots == column, total[:, :HALF], jnp.where(spots == column + TILE, total[:, HALF:], 0.0))
    return jnp.sum(hit, axis=0, keepdims=True)


def momentum_pick_kernel(
    place, momentum, gate, up, row_pair, band, offsets, piece, out, gate_held, up_held, gated, upper, grads,
    held, twice, stack, incoming, arrived,
):
    steps, rows, span = held.shape

    def load(step):
        return pltpu.make_async_copy(momentum.at[0, :, pl.ds(step * span, span)], held.at[step], incoming.at[step])

    for step in range(steps):
        load(step).start()
    weights = weight_loads(place, gate, up, gate_held, up_held, arrived)
    for weight in weights:
        weight.start()
    twice[...] = jnp.zeros_like(twice)
    bands = jnp.concatenate([band[...], band[:, :BAND]], axis=1)
    for step in range(steps):
        load(step).wait()
        turned = held[step].T
        twice[:, :rows] = turned
        twice[:, 2 * HALF : 2 * HALF + rows] = turned
        high, low = split(BETA_DECAY * dot(twice[...], row_pair[...]))
        for start in range(0, span, BAND):
            stack[:BAND] = high[start : start + BAND]
            stack[BAND : 2 * BAND] = high[start : start + BAND]
            stack[2 * BAND :] = low[start : start + BAND]
            total = dot(bands, stack[...])
            for k in range(BAND // TILE):
                tile = (step * span + start) // TILE + k
                spots = offsets[place[1], tile : tile + 1, :]
                out[tile : tile + 1, :] = picked(total[k * TILE : (k + 1) * TILE], spots)
    for weight in weights:
        weight.wait()
    feature = piece_features(piece, gated.shape[1])
    gated[...] = dot(gate_held[0], feature)
    upper[...] = dot(up_held[0], feature)
    piece_grads(piece, band, grads)


def piece_features(piece, columns):
    depth, lines, count = piece.shape
    features = 2 * lines // 5
    next_count = columns - count
    packed = piece[:, 2 * features :].astype(F32)
    blocks = []
    for d in range(depth):
        blocks += [packed[d, :, :next_count], packed[d, :, next_count:]]
    nexts = jnp.concatenate(blocks, axis=0).astype(BF16)
    return jnp.concatenate([piece[:, :features].reshape(depth * features, count), nexts], axis=1)


def piece_grads(piece, band, grads):
    depth, lines, count = piece.shape
    features = 2 * lines // 5
    width = depth * features
    block = piece[:, features : 2 * features].reshape(width, count)
    for start in range(0, width, BAND):
        size = min(BAND, width - start)
        part = block[start : start + size]
        high, low = split(dot(band[:size, :size], part) + dot(band[:size, BAND : BAND + size], part))
        grads[start : start + size, :count] = high
        grads[start : start + size, count : 2 * count] = low
        grads[start : start + size, 2 * count :] = high


def weight_loads(place, gate, up, gate_held, up_held, arrived):
    width = gate.shape[1] // RING
    loads = []
    for step in range(RING):
        owner = lax.rem(place[0] + RING - step, RING)
        columns = pl.ds(pl.multiple_of(owner * width, 128), width)
        loads.append(pltpu.make_async_copy(gate.at[:, columns], gate_held.at[step], arrived.at[2 * step]))
        loads.append(pltpu.make_async_copy(up.at[:, columns], up_held.at[step], arrived.at[2 * step + 1]))
    return loads


def ring_swiglu(gated, upper, features, gate_held, up_held):
    for step, feature in enumerate(features):
        gated = gated + dot(gate_held[step + 1], feature)
        upper = upper + dot(up_held[step + 1], feature)
    return (gated / (1.0 + jnp.exp(-gated)) * upper).astype(BF16)


def pick_kernel(place, *refs):
    pieces = refs[:RING]
    gate_held, up_held, row_pair, band, momentum_part, offsets = refs[RING : RING + 6]
    own_gated, own_upper, own_grads = refs[RING + 6 : RING + 9]
    refs = refs[3:]
    whole_grads, hidden, next_hidden, sent = refs[RING + 6 : RING + 10]
    grads, total, factor, rows_held, units, next_units, coefficients, packed_held, rows_arrived, left = refs[RING + 10 :]
    rows, count = hidden.shape
    next_count = next_hidden.shape[1]
    depth, features = pieces[0].shape[0], whole_grads.shape[1]
    width = depth * features
    owners = [lax.rem(place[0] + RING - step, RING) for step in range(RING)]
    rows_load = pltpu.make_async_copy(row_pair, rows_held, rows_arrived.at[0])
    rows_load.start()
    stores = [
        pltpu.make_async_copy(
            piece.at[:, features : 2 * features], whole_grads.at[pl.ds(owners[step] * depth, depth)], left.at[step]
        )
        for step, piece in enumerate(pieces)
    ]
    for store in stores:
        store.start()

    for step, piece in enumerate(pieces[1:]):
        piece_grads(piece, band, grads.at[step * width : (step + 1) * width])
    columns = count + next_count
    feature_blocks = [piece_features(piece, columns) for piece in pieces[1:]]
    turned = ring_swiglu(own_gated[...], own_upper[...], feature_blocks, gate_held, up_held)
    units[...] = turned[:, :count]
    next_units[...] = turned[:, count:]
    for source, target in ((units, hidden), (next_units, next_hidden)):
        stores.append(pltpu.make_async_copy(source, target, left.at[len(stores)]))
        stores[-1].start()
    turned = turned[:, :count].T
    rows_load.wait()
    high, low = split(dot(turned, rows_held[:rows]) + dot(turned, rows_held[2 * HALF : 2 * HALF + rows]))
    factor[:count] = high
    factor[count : 2 * count] = high
    factor[2 * count :] = low

    for step in range(RING):
        part = own_grads[...] if step == 0 else grads[(step - 1) * width : step * width]
        total[...] = dot(part, factor[...])
        for k in range(width // TILE):
            tile = owners[step] * (width // TILE) + k
            row = pl.ds(tile, 1)
            spots = offsets[place[1], row, :]
            coefficients[row, :] = picked(total[k * TILE : (k + 1) * TILE], spots) + momentum_part[row, :]
    value = coefficients[...]
    packed_held[...] = jnp.concatenate([value[:, : HALF // 2], value[:, HALF // 2 :]], axis=0).astype(BF16)
    for target in [sent.at[r] for r in range(sent.shape[0])]:
        stores.append(pltpu.make_async_copy(packed_held, target, left.at[len(stores)]))
        stores[-1].start()
    for store in stores:
        store.wait()


def next_kernel(next_hidden, down, row_pair, base, factor, down_held, base_held, down_arrived, base_left):
    rows = down.shape[0]
    bands = down_held.shape[0]
    span = down_held.shape[2]
    loads = [
        pltpu.make_async_copy(down.at[:, pl.ds(step * span, span)], down_held.at[step], down_arrived.at[step])
        for step in range(bands)
    ]
    for load in loads:
        load.start()
    turned = next_hidden[...].T
    along = (dot(turned, row_pair[:rows]) + dot(turned, row_pair[2 * HALF : 2 * HALF + rows])).T
    factor[...] = jnp.concatenate(split(along), axis=1)
    for step, load in enumerate(loads):
        load.wait()
        base_held[:, step * span : (step + 1) * span] = dot(turned, down_held[step])
    store = pltpu.make_async_copy(base_held, base.at[: turned.shape[0]], base_left.at[0])
    store.start()
    store.wait()


def output_kernel(
    values, offsets, next_rows, base_whole, back, out,
    base, dense, across, rearranged, columns, even_values, odd_values, base_arrived,
):
    replicas, tile_cols, _ = offsets.shape
    tokens = base.shape[0]
    base_load = pltpu.make_async_copy(base_whole.at[:tokens], base, base_arrived.at[0])
    base_load.start()
    bands = base.shape[1] // BAND
    chunks = base.shape[1] // 128
    for r in range(replicas):
        value = values[r].astype(F32)
        value = jnp.concatenate([value[:tile_cols], value[tile_cols:]], axis=1)
        columns[r] = (offsets[r] & (TILE - 1)).astype(F32)
        even_values[r] = jnp.where(offsets[r] < TILE, value, 0.0)
        odd_values[r] = jnp.where(offsets[r] < TILE, 0.0, value)
    place = lax.broadcasted_iota(jnp.int32, (TILE, 128), 0).astype(F32).astype(BF16)
    zero = jnp.zeros((PACK, 128), BF16)

    def one(tile, carry):
        for start in range(0, HALF, 128):
            listed = []
            for r in range(replicas):
                rows = (table[r, pl.ds(tile, 1), :][:, start : start + 128] for table in (columns, even_values, odd_values))
                listed.append([jnp.broadcast_to(row, (PACK, 128)).astype(BF16) for row in rows])
            for first in range(0, TILE, PACK):
                even, odd = zero, zero
                for spots, even_value, odd_value in listed:
                    hit = spots == place[first : first + PACK]
                    even += jnp.where(hit, even_value, zero)
                    odd += jnp.where(hit, odd_value, zero)
                row = pl.ds(pl.multiple_of(tile * TILE + first, PACK), PACK)
                dense[row, start : start + 128] = even
                dense[row, HALF + start : HALF + start + 128] = odd
        return carry

    lax.fori_loop(0, tile_cols, one, 0, unroll=4)
    for step in range(0, bands, 2):
        both = dot(dense[step * BAND : (step + 2) * BAND], next_rows[...]).astype(BF16)
        for k in range(2):
            part = both[k * BAND : (k + 1) * BAND]
            across[:BAND, (step + k) * 128 : (step + k + 1) * 128] = part
            across[BAND:, (step + k) * 128 : (step + k + 1) * 128] = part
    change = dot(back[...], across[...])
    base_load.wait()
    for step in range(bands):
        turned = change[:, step * 128 : (step + 1) * 128].T
        result = base[:, step * BAND : (step + 1) * BAND] - (STEP_RATE / replicas) * (turned[:tokens] + turned[tokens:])
        for c in range(BAND // 128):
            rearranged[pl.ds(step * (BAND // 128) + c, tokens, stride=chunks), :] = result[:, c * 128 : (c + 1) * 128]
    out[...] = rearranged[...].astype(BF16)


def kept_kernel(
    place, sent, offsets, whole_grads, hidden, momentum, row_pair, back, out,
    own, cotangent, held, ready, dense, left, right, incoming, outgoing, grads_arrived,
):
    steps, rows, span = held.shape
    spectral = 2 * HALF

    def load(step):
        return pltpu.make_async_copy(momentum.at[0, :, pl.ds(step * span, span)], held.at[step], incoming.at[step])

    def store(step):
        return pltpu.make_async_copy(ready.at[step], out.at[0, :, pl.ds(step * span, span)], outgoing.at[step])

    grads_load = pltpu.make_async_copy(whole_grads.at[: cotangent.shape[0]], cotangent, grads_arrived.at[0])
    grads_load.start()
    for step in range(steps):
        load(step).start()
    value = sent[0].astype(F32)
    own[...] = jnp.concatenate([value[: own.shape[0]], value[own.shape[0] :]], axis=1)
    left[:, :spectral] = row_pair[:rows]
    left[:, spectral : 2 * spectral] = row_pair[:rows]
    left[:, 2 * spectral : 3 * spectral] = row_pair[spectral : spectral + rows]
    left[:, 3 * spectral :] = -hidden[...]
    column = lax.broadcasted_iota(jnp.int32, (TILE, HALF), 0)
    grads_load.wait()
    grads = cotangent[...].reshape(steps * span, cotangent.shape[2])
    for step in range(steps):
        for start in range(0, span, BAND):
            for k in range(BAND // TILE):
                tile = (step * span + start) // TILE + k
                spots, value = offsets[place[1], tile : tile + 1, :], own[tile : tile + 1, :]
                even = jnp.where(spots == column, value, 0.0).astype(BF16)
                odd = jnp.where(spots == column + TILE, value, 0.0).astype(BF16)
                for copy in range(2):
                    dense[copy * BAND + k * TILE : copy * BAND + (k + 1) * TILE, :HALF] = even
                    dense[copy * BAND + k * TILE : copy * BAND + (k + 1) * TILE, HALF:] = odd
            high, low = split(dot(back[...], dense[...]))
            right[start : start + BAND, :spectral] = high
            right[start : start + BAND, spectral : 2 * spectral] = low
            right[start : start + BAND, 2 * spectral : 3 * spectral] = high
        right[:, 3 * spectral :] = grads[step * span : (step + 1) * span]
        change = dot_turned(left[...], right[...])
        load(step).wait()
        ready[step] = (BETA_DECAY * held[step].astype(F32) - change).astype(BF16)
        store(step).start()
    for step in range(steps):
        store(step).wait()


def sum_kernel(received, out):
    total = jnp.sum(received[...].astype(F32), axis=0)
    chunks = out.shape[1] // 128
    lines = [
        jnp.concatenate([total[h * chunks + c : h * chunks + c + 1] for c in range(chunks)], axis=1)
        for h in range(out.shape[0])
    ]
    out[...] = jnp.concatenate(lines, axis=0).astype(BF16)


IN_VMEM = pl.BlockSpec(memory_space=pltpu.VMEM)
IN_SMEM = pl.BlockSpec(memory_space=pltpu.SMEM)
IN_HBM = pl.BlockSpec(memory_space=pltpu.HBM)


def params(limit=36):
    return pltpu.CompilerParams(vmem_limit_bytes=limit * 1024 * 1024)


def cost(flops, moved):
    return pl.CostEstimate(flops=int(flops), bytes_accessed=int(moved), transcendentals=0)


def depth_gather(block, depth):
    groups = [[x * depth + z for z in range(depth)] for x in range(RING)]
    return lax.all_to_all(block, "tensor", 0, 0, tiled=True, axis_index_groups=groups)


def ring_gather(block, depth):
    pieces = [block]
    for step in range(1, RING):
        pairs = [(x * depth + z, (x + step) % RING * depth + z) for x in range(RING) for z in range(depth)]
        pieces.append(lax.ppermute(block, "tensor", pairs))
    return pieces


def on_device(tokens, next_tokens, cotangent, gate_weight, up_weight, down_weight, momentum, indices):
    shards = lax.axis_size("tensor")
    depth = shards // RING
    replicas = lax.axis_size("replica")
    place = jnp.stack([lax.axis_index("tensor") // depth, lax.axis_index("replica")]).astype(jnp.int32)
    rows, width = down_weight.shape
    bands = width // BAND
    part = width // RING
    tile_rows, tile_cols, keep = indices.shape[1:]
    stride = TILE * TILE // keep
    count, next_count, features = tokens.shape[0], next_tokens.shape[0], tokens.shape[1]
    row_pair = jnp.asarray(np.concatenate(parts(row_table(rows))))
    band = jnp.asarray(np.concatenate(parts(band_table()), axis=1))
    back = jnp.asarray(np.concatenate(parts(band_table().T), axis=1))
    gate, up = gate_weight.T, up_weight.T

    packed = pl.pallas_call(
        pack_kernel,
        in_specs=[IN_VMEM] * 3,
        out_specs=IN_VMEM,
        out_shape=jax.ShapeDtypeStruct((depth, 2 * features + features // 2, count), BF16),
        compiler_params=params(58),
        name="pack",
    )(tokens.T, cotangent.T, next_tokens)
    pieces = ring_gather(depth_gather(packed, depth), depth)

    offsets = indices - jnp.arange(keep, dtype=jnp.int32) * stride
    offsets = offsets.transpose(0, 2, 1, 3).reshape(replicas, tile_cols, tile_rows * keep)
    offsets = jnp.pad(offsets, ((0, 0), (0, 0), (0, HALF - tile_rows * keep)), constant_values=-1)

    def shape(dims, kind):
        return jax.ShapeDtypeStruct(dims, kind)

    dma = pltpu.SemaphoreType.DMA

    momentum_part, gate_held, up_held, *own_parts = pl.pallas_call(
        momentum_pick_kernel,
        in_specs=[IN_SMEM] + [IN_HBM] * 3 + [IN_VMEM] * 4,
        out_specs=[IN_VMEM] * 6,
        out_shape=[shape((tile_cols, HALF), F32)]
        + [shape((RING, rows, part), BF16)] * 2
        + [shape((rows, count + next_count), F32)] * 2
        + [shape((part, 3 * count), BF16)],
        scratch_shapes=[
            pltpu.VMEM((width // SPAN, rows, SPAN), BF16),
            pltpu.VMEM((SPAN, 4 * HALF), BF16),
            pltpu.VMEM((3 * BAND, 2 * HALF), BF16),
            dma((width // SPAN,)),
            dma((2 * RING,)),
        ],
        compiler_params=params(36),
        cost_estimate=cost(6e9, 8e6),
        name="momentum_pick",
    )(place, momentum, gate, up, row_pair, band, offsets, pieces[0])

    whole_grads, hidden, next_hidden, sent = pl.pallas_call(
        pick_kernel,
        in_specs=[IN_SMEM] + [IN_VMEM] * (RING + 2) + [IN_HBM] + [IN_VMEM] * 6,
        out_specs=[IN_HBM] * 4,
        out_shape=[
            shape((ROOM // (features * count * 2), features, count), BF16),
            shape((rows, count), BF16),
            shape((rows, next_count), BF16),
            shape((replicas, 2 * tile_cols, HALF // 2), BF16),
        ],
        scratch_shapes=[
            pltpu.VMEM((width - part, 3 * count), BF16),
            pltpu.VMEM((part, 2 * HALF), F32),
            pltpu.VMEM((3 * count, 2 * HALF), BF16),
            pltpu.VMEM((4 * HALF, 2 * HALF), BF16),
            pltpu.VMEM((rows, count), BF16),
            pltpu.VMEM((rows, next_count), BF16),
            pltpu.VMEM((tile_cols, HALF), F32),
            pltpu.VMEM((2 * tile_cols, HALF // 2), BF16),
            dma((1,)),
            dma((RING + 2 + replicas,)),
        ],
        compiler_params=params(36),
        cost_estimate=cost(6e9, 12e6),
        name="pick",
    )(place, *pieces, gate_held, up_held, row_pair, band, momentum_part, offsets, *own_parts)

    listed = lax.all_to_all(sent, "replica", 0, 0, tiled=True)

    base, next_rows = pl.pallas_call(
        next_kernel,
        in_specs=[IN_VMEM, IN_HBM, IN_VMEM],
        out_specs=[IN_HBM, IN_VMEM],
        out_shape=[shape((ROOM // (width * 4), width), F32), shape((2 * HALF, 2 * next_count), BF16)],
        scratch_shapes=[
            pltpu.VMEM((width // SPAN, rows, SPAN), BF16),
            pltpu.VMEM((next_count, width), F32),
            dma((width // SPAN,)),
            dma((1,)),
        ],
        compiler_params=params(),
        cost_estimate=cost(2e9, 7e6),
        name="next_rows",
    )(next_hidden, down_weight, row_pair)

    partial = pl.pallas_call(
        output_kernel,
        in_specs=[IN_VMEM] * 3 + [IN_HBM, IN_VMEM],
        out_specs=IN_VMEM,
        out_shape=shape((next_count * width // 128, 128), BF16),
        scratch_shapes=[
            pltpu.VMEM((next_count, width), F32),
            pltpu.VMEM((width, 2 * HALF), BF16),
            pltpu.VMEM((2 * BAND, bands * 2 * next_count), BF16),
            pltpu.VMEM((next_count * width // 128, 128), F32),
        ]
        + [pltpu.VMEM((replicas, tile_cols, HALF), F32)] * 3
        + [dma((1,))],
        compiler_params=params(),
        cost_estimate=cost(4e9, 4e6),
        name="output_part",
    )(listed, offsets, next_rows, base, back)

    received = lax.all_to_all(partial.reshape(shards, -1, 128), "tensor", 0, 0, tiled=True)
    output = pl.pallas_call(
        sum_kernel,
        in_specs=[IN_VMEM],
        out_specs=IN_VMEM,
        out_shape=shape((next_count // shards, width), BF16),
        compiler_params=params(),
        name="output_sum",
    )(received)

    kept = pl.pallas_call(
        kept_kernel,
        in_specs=[IN_SMEM, IN_VMEM, IN_VMEM, IN_HBM, IN_VMEM, IN_HBM, IN_VMEM, IN_VMEM],
        out_specs=IN_HBM,
        out_shape=shape((1, rows, width), BF16),
        scratch_shapes=[pltpu.VMEM((tile_cols, HALF), F32), pltpu.VMEM((shards, features, count), BF16)]
        + [pltpu.VMEM((width // SPAN, rows, SPAN), BF16)] * 2
        + [
            pltpu.VMEM((2 * BAND, 2 * HALF), BF16),
            pltpu.VMEM((rows, 6 * HALF + count), BF16),
            pltpu.VMEM((SPAN, 6 * HALF + count), BF16),
            dma((width // SPAN,)),
            dma((width // SPAN,)),
            dma((1,)),
        ],
        compiler_params=params(),
        cost_estimate=cost(10e9, 8e6),
        name="kept",
    )(place, sent, offsets, whole_grads, hidden, momentum, row_pair, back)
    return (output, kept)


def solution(mesh):
    return jax.shard_map(
        on_device,
        mesh=mesh,
        in_specs=(
            P("replica", "tensor"),
            P("replica", "tensor"),
            P("replica", "tensor"),
            P(None, "tensor"),
            P(None, "tensor"),
            P("tensor", None),
            P("replica", "tensor", None),
            P(None, "tensor", None, None),
        ),
        out_specs=(P(("replica", "tensor"), None), P("replica", "tensor", None)),
        check_vma=False,
    )
```
